32 devices in a mesh: gx: 2 (over core), gy: 4 (over y, x), af: 4 (over z).
Axes of the slice: x: 2, y: 2, z: 4, core: 2. Of those that a mesh axis runs over, the one named last changes fastest.
Arguments:
- features: bfloat16 [8192, 1024], P(('gx', 'gy'), 'af'), may hold values from -6 to 6
- adj_tiles: bfloat16 [64, 4, 128, 128], P(('gx', 'gy')), may hold values from -0.25 to 0.25
- col_block: int32 [64, 4], P(('gx', 'gy')), may hold values from 0 to 7, as said below
- send_rows: int32 [32, 384], P(('gx', 'gy')), may hold values from 0 to 1023
- send_counts: int32 [32], P(('gx', 'gy')), may hold values from 96 to 384, as said below
- recv_target: int32 [32, 384], P(('gx', 'gy')), may hold values from 0 to 1023
- edge_weight: float32 [32, 384], P(('gx', 'gy')), may hold values from -3 to 3
- labels: int32 [8192], P(('gx', 'gy')), may hold values from 0 to 127
- w_hidden: bfloat16 [1024, 1024], P('af'), may hold values from -0.1875 to 0.1875
- w_classes: bfloat16 [1024, 128], P('af'), may hold values from -0.5 to 0.5
Outputs:
- grad_w_hidden: float32 [1024, 1024], P('af')
- grad_w_classes: float32 [1024, 128], P('af')
The draws below stay inside these ranges and needn't reach their ends.
Inputs may be any that keep to these rules, and one draw needn't show every extreme that they name: `send_counts`: entry 4 p + d is the number of leading live slots in row 4 p + d of send_rows; some entry equals 384. `col_block`: entry k = 0 of row t is t mod (8), the tile's own block; the 4 entries of a row are distinct. `send_rows`: rows of the sending partition; repeats possible. `recv_target`: rows of the receiving partition; repeats possible.
All inputs are finite; a program needn't handle non-finite values.
Results may differ from the reference program's by a relative error of at most 0.008.
Values may be sent and summed in bfloat16 or wider, within the bound.
A program may use at most 64 MiB of HBM per device.

```python
import jax
import jax.numpy as jnp
from jax import lax

D = 1024
H = 1024
C = 128
NODES = 1024
TB = 128
KT = 4
S = 384
PARTITIONS = 8
NODES_ALL = 8192
BLOCKS_ALL = 64
N_GX = 2
N_GY = 4


def draw_col_block(key, part):
    blocks = NODES // TB
    column_ids = jnp.arange(blocks, dtype=jnp.int32)
    scores = jax.random.randint(key, (BLOCKS_ALL, blocks), 0, 1 << 20, dtype=jnp.int32) * blocks + column_ids[None, :]
    own_block = jnp.arange(BLOCKS_ALL, dtype=jnp.int32) % blocks
    scores = jnp.where(column_ids[None, :] == own_block[:, None], -1, scores)
    ranking = jnp.argsort(scores, axis=1, stable=True)
    return ranking[:, :KT].astype(jnp.int32)


def draw_send_counts(key, part):
    count_key, pick_key = jax.random.split(key)
    counts = jax.random.randint(count_key, (4 * PARTITIONS,), max(1, S // 4), S + 1, dtype=jnp.int32)
    chosen = jax.random.randint(pick_key, (), 0, 4 * PARTITIONS, dtype=jnp.int32)
    return jnp.where(jnp.arange(4 * PARTITIONS, dtype=jnp.int32) == chosen, S, counts).astype(jnp.int32)


def set_ends(drawn, stream_key, smallest, top_value):
    index_at = [jax.random.randint(jax.random.fold_in(stream_key, axis), (), 0, length) for axis, length in enumerate(drawn.shape)]
    widest = drawn.shape.index(max(drawn.shape))
    beside = index_at[:widest] + [(index_at[widest] + 1) % drawn.shape[widest]] + index_at[widest + 1:]
    return drawn.at[tuple(index_at)].set(smallest).at[tuple(beside)].set(top_value)


def levels(own_key, shape, pieces, smallest, top_value):
    loudness = 1.0
    for dim, blocks in pieces:
        draws = jax.random.uniform(jax.random.fold_in(jax.random.fold_in(own_key, 6), dim), (blocks,), jnp.float32, smallest / len(pieces), top_value / len(pieces))
        loudness = loudness * jnp.repeat(jnp.exp(draws), shape[dim] // blocks).reshape((-1,) + (1,) * (len(shape) - 1 - dim))
    return loudness


def scatter_about(stream_key, extent, scale, bound, pieces=(), held_as=jnp.bfloat16):
    result = jax.random.normal(stream_key, extent, jnp.float32) * scale
    if len(pieces) > 0:
        result = levels(stream_key, extent, pieces, -0.22, 0.18) * result
    return jnp.clip(result, min=-bound, max=bound).astype(held_as)


def setup_inputs(seed: int = 0) -> dict:
    key_list = jax.random.split(jax.random.key(seed), 11)
    features = scatter_about(key_list[0], (NODES_ALL, D), 1.0, 6.0, ((0, 8), (1, 4)))
    adj_tiles = scatter_about(key_list[1], (BLOCKS_ALL, KT, TB, TB), (KT * TB) ** -0.5, 0.25, ((0, 8),))
    col_block = draw_col_block(jax.random.fold_in(key_list[10], 71), 0)
    send_rows = set_ends(jax.random.randint(key_list[3], (4 * PARTITIONS, S), 0, NODES), jax.random.fold_in(key_list[3], 1), 0, NODES - 1).astype(jnp.int32)
    send_counts = draw_send_counts(jax.random.fold_in(key_list[10], 71), 0)
    recv_target = set_ends(jax.random.randint(key_list[5], (4 * PARTITIONS, S), 0, NODES), jax.random.fold_in(key_list[5], 1), 0, NODES - 1).astype(jnp.int32)
    edge_weight = scatter_about(key_list[6], (4 * PARTITIONS, S), 1.0, 3.0, ((0, 8),), jnp.float32)
    labels = set_ends(jax.random.randint(key_list[7], (NODES_ALL,), 0, C), jax.random.fold_in(key_list[7], 1), 0, C - 1).astype(jnp.int32)
    w_hidden = scatter_about(key_list[8], (D, H), D ** -0.5, 0.1875, ((0, 4),))
    w_classes = scatter_about(key_list[9], (H, C), (H // 9) ** -0.5, 0.5, ((0, 4),))
    return {"features": features, "adj_tiles": adj_tiles, "col_block": col_block, "send_rows": send_rows, "send_counts": send_counts, "recv_target": recv_target, "edge_weight": edge_weight, "labels": labels, "w_hidden": w_hidden, "w_classes": w_classes}


def aggregate(node_field, adj_tiles, col_block, send_rows, send_counts, recv_target, edge_weight):
    feat_width = node_field.shape[1]
    blocks = NODES // TB
    parts_count = N_GX * N_GY
    local_field = node_field.reshape(parts_count, blocks, TB, feat_width)
    tile_view = adj_tiles.reshape(parts_count, blocks, KT, TB, TB)
    index_view = col_block.reshape(parts_count, blocks, KT)

    def one_part(operands):
        part_field, part_tiles, part_index = operands
        picked = part_field[part_index]
        summed = jnp.einsum("bkij,bkjf->bif", part_tiles.astype(jnp.float32), picked.astype(jnp.float32))
        return summed.reshape(NODES, feat_width)

    local_sum = lax.map(one_part, (local_field, tile_view, index_view)).reshape(parts_count * NODES, feat_width)
    slot_ids = jnp.arange(S, dtype=jnp.int32)
    slot_live = slot_ids[None, :] < send_counts[:, None]
    part_base = (jnp.arange(4 * parts_count, dtype=jnp.int32) // 4) * NODES
    outgoing = node_field[part_base[:, None] + send_rows]
    outgoing = jnp.where(slot_live[:, :, None], outgoing, jnp.zeros((), node_field.dtype))
    grid_out = outgoing.reshape(N_GX, N_GY, 4, S, feat_width)
    zero_row = jnp.zeros_like(grid_out[:1, :, 0])
    zero_col = jnp.zeros_like(grid_out[:, :1, 0])
    from_lower_x = jnp.concatenate([zero_row, grid_out[:-1, :, 0]], 0)
    from_upper_x = jnp.concatenate([grid_out[1:, :, 1], zero_row], 0)
    from_lower_y = jnp.concatenate([zero_col, grid_out[:, :-1, 2]], 1)
    from_upper_y = jnp.concatenate([grid_out[:, 1:, 3], zero_col], 1)
    arrived = jnp.stack([from_lower_x, from_upper_x, from_lower_y, from_upper_y], 2)
    arrived = arrived.reshape(4 * parts_count, S, feat_width)
    weighted = edge_weight[:, :, None] * arrived.astype(jnp.float32)
    targets = part_base[:, None] + recv_target
    return local_sum.at[targets.reshape(-1)].add(weighted.reshape(-1, feat_width))


def aggregate_back(grad_field, adj_tiles, col_block, send_rows, send_counts, recv_target, edge_weight):
    feat_width = grad_field.shape[1]
    blocks = NODES // TB
    parts_count = N_GX * N_GY
    local_grad = grad_field.reshape(parts_count, blocks, TB, feat_width)
    tile_view = adj_tiles.reshape(parts_count, blocks, KT, TB, TB)
    index_view = col_block.reshape(parts_count, blocks, KT)

    def one_part(operands):
        part_grad, part_tiles, part_index = operands
        spread = jnp.einsum("bkij,bif->bkjf", part_tiles.astype(jnp.float32), part_grad.astype(jnp.float32))
        placed = jnp.zeros((blocks, TB, feat_width), jnp.float32)
        placed = placed.at[part_index.reshape(-1)].add(spread.reshape(blocks * KT, TB, feat_width))
        return placed.reshape(NODES, feat_width)

    local_sum = lax.map(one_part, (local_grad, tile_view, index_view)).reshape(parts_count * NODES, feat_width)
    slot_ids = jnp.arange(S, dtype=jnp.int32)
    slot_live = slot_ids[None, :] < send_counts[:, None]
    part_base = (jnp.arange(4 * parts_count, dtype=jnp.int32) // 4) * NODES
    gathered = grad_field[part_base[:, None] + recv_target].astype(jnp.float32)
    back_terms = (edge_weight[:, :, None] * gathered).astype(jnp.bfloat16)
    grid_back = back_terms.reshape(N_GX, N_GY, 4, S, feat_width)
    zero_row = jnp.zeros_like(grid_back[:1, :, 0])
    zero_col = jnp.zeros_like(grid_back[:, :1, 0])
    return_zero = jnp.concatenate([grid_back[1:, :, 0], zero_row], 0)
    return_one = jnp.concatenate([zero_row, grid_back[:-1, :, 1]], 0)
    return_two = jnp.concatenate([grid_back[:, 1:, 2], zero_col], 1)
    return_three = jnp.concatenate([zero_col, grid_back[:, :-1, 3]], 1)
    returned = jnp.stack([return_zero, return_one, return_two, return_three], 2)
    returned = returned.reshape(4 * parts_count, S, feat_width).astype(jnp.float32)
    returned = jnp.where(slot_live[:, :, None], returned, jnp.zeros((), jnp.float32))
    sources = part_base[:, None] + send_rows
    return local_sum.at[sources.reshape(-1)].add(returned.reshape(-1, feat_width))


def reference(features, adj_tiles, col_block, send_rows, send_counts, recv_target, edge_weight, labels, w_hidden, w_classes):
    graph_parts = (adj_tiles, col_block, send_rows, send_counts, recv_target, edge_weight)
    mixed_in = aggregate(features, *graph_parts).astype(jnp.bfloat16)
    pre_act = jnp.dot(mixed_in, w_hidden, preferred_element_type=jnp.float32)
    hidden = jax.nn.silu(pre_act).astype(jnp.bfloat16)
    mixed_hidden = aggregate(hidden, *graph_parts).astype(jnp.bfloat16)
    logits = jnp.dot(mixed_hidden, w_classes, preferred_element_type=jnp.float32)
    exponent = jnp.exp(logits - jnp.max(logits, axis=1, keepdims=True))
    probability = exponent / jnp.sum(exponent, axis=1, keepdims=True)
    onehot = (labels[:, None] == jnp.arange(C, dtype=jnp.int32)[None, :]).astype(jnp.float32)
    grad_logits = ((probability - onehot) / 64.0).astype(jnp.bfloat16)
    grad_classes = jnp.dot(mixed_hidden.T, grad_logits, preferred_element_type=jnp.float32)
    grad_mixed = jnp.dot(grad_logits, w_classes.T, preferred_element_type=jnp.float32).astype(jnp.bfloat16)
    grad_act = aggregate_back(grad_mixed, *graph_parts)
    sigmoid_act = jax.nn.sigmoid(pre_act)
    grad_pre = (grad_act * sigmoid_act * (1.0 + pre_act * (1.0 - sigmoid_act))).astype(jnp.bfloat16)
    grad_hidden = jnp.dot(mixed_in.T, grad_pre, preferred_element_type=jnp.float32)
    return (grad_hidden, grad_classes)
```

```python
import functools

import jax
import jax.numpy as jnp
from jax import lax
from jax.experimental import pallas as pl
from jax.experimental.pallas import tpu as pltpu
from jax.sharding import PartitionSpec as P

MESH = pl.DeviceIdType.MESH
BF = jnp.bfloat16
F32 = jnp.float32
CHUNKS = 4


def mm(a, b):
    return jnp.dot(a, b, preferred_element_type=F32)


def mm_tn(a, b):
    return lax.dot_general(a, b, (((0,), (0,)), ((), ())), preferred_element_type=F32)


def mm_nt(a, b):
    return lax.dot_general(a, b, (((1,), (1,)), ((), ())), preferred_element_type=F32)


def kernel(
    sizes,
    feat,
    adj,
    colb,
    row_i,
    col_i,
    col_w,
    labels,
    wh,
    wc,
    out_w,
    out_c,
    send_hot,
    send_hot_t,
    recv_hot,
    recv_hot_t,
    dense,
    dense_t,
    acc,
    field,
    halo_out,
    halo_in,
    gathered,
    w_cols,
    pre,
    mixed_hidden,
    logit_out,
    logit_in,
    grad_logits,
    grad_out,
    grad_in,
    class_out,
    class_in,
    piece_out,
    piece_in,
    whole_w,
    whole_c,
    halo_ss,
    halo_rs,
    up_ss,
    down_ss,
    ag_rs,
    w_ss,
    w_rs,
    lo_ss,
    lo_rs,
    gl_ss,
    gl_rs,
    rs_ss,
    rs_rs,
    cr_ss,
    cr_rs,
    za_ss,
    za_rs,
    fw_ss,
    fw_rs,
    fc_ss,
    fc_rs,
):
    gx, gy, af = sizes
    nodes, width = feat.shape
    slots = col_i.shape[0] // 4
    parts = gx * gy
    rows = width // parts
    quarter = nodes // af
    step = nodes // CHUNKS
    classes = wc.shape[1]
    blocks, tiles, tb, _ = adj.shape
    ix, iy, z = lax.axis_index("gx"), lax.axis_index("gy"), lax.axis_index("af")
    me = ix * gy + iy

    def plane_peer(k):
        px = lax.rem(ix + k // gy, gx)
        py = lax.rem(iy + k % gy, gy)
        return px, py

    def af_peer(k):
        return lax.rem(z + k, af)

    def remote(src, dst, ss, rs, where):
        return pltpu.make_async_remote_copy(
            src_ref=src, dst_ref=dst, send_sem=ss, recv_sem=rs, device_id=where, device_id_type=MESH
        )

    barrier = pltpu.get_barrier_semaphore()
    for k in range(1, parts):
        px, py = plane_peer(k)
        pl.semaphore_signal(barrier, inc=1, device_id=(px, py, z), device_id_type=MESH)
    for k in range(1, af):
        pl.semaphore_signal(barrier, inc=1, device_id=(ix, iy, af_peer(k)), device_id_type=MESH)

    def build_rows(hot, column):
        @pl.loop(0, 4 * slots // 32)
        def _(i):
            at = pl.ds(pl.multiple_of(i * 32, 32), 32)
            ids = col_i[at, column : column + 1]
            lane = lax.broadcasted_iota(jnp.int32, (32, nodes), 1)
            hot[at, :] = jnp.where(lane == ids, 1.0, 0.0).astype(BF)

    def build_cols(hot, row):
        @pl.loop(0, nodes // 32)
        def _(i):
            at = pl.ds(pl.multiple_of(i * 32, 32), 32)
            node = lax.broadcasted_iota(jnp.int32, (32, 4 * slots), 0) + i * 32
            hot[at, :] = jnp.where(node == row_i[row : row + 1, :], 1.0, 0.0).astype(BF)

    build_rows(send_hot, 0)
    pl.semaphore_wait(barrier, parts - 1 + af - 1)

    for k in range(1, af):
        there = af_peer(k)
        remote(
            wh.at[:, pl.ds(pl.multiple_of(there * width, width), width)],
            w_cols.at[z],
            w_ss.at[k],
            w_rs.at[k],
            (ix, iy, there),
        ).start()
    w_cols[z] = wh[:, pl.ds(pl.multiple_of(z * width, width), width)]

    ahead = ((ix + 1 < gx), (ix > 0), (iy + 1 < gy), (iy > 0))
    behind = ((ix > 0), (ix + 1 < gx), (iy > 0), (iy + 1 < gy))
    ahead_id = ((ix + 1, iy, z), (ix - 1, iy, z), (ix, iy + 1, z), (ix, iy - 1, z))
    behind_id = ((ix - 1, iy, z), (ix + 1, iy, z), (ix, iy - 1, z), (ix, iy + 1, z))

    def halo_copy(turn, d, ids):
        return remote(
            halo_out.at[turn, d], halo_in.at[turn, d], halo_ss.at[turn, d], halo_rs.at[turn, d], ids[d]
        )

    def halo_send(turn, source, hot, weighted, targets, ids):
        for d in range(4):
            picked = mm(hot[d * slots : (d + 1) * slots, :], source[...])
            if weighted:
                picked = picked * col_w[d * slots : (d + 1) * slots, :]
            halo_out[turn, d] = picked.astype(BF)

            @pl.when(targets[d])
            def _():
                halo_copy(turn, d, ids).start()

    def halo_take(turn, hot_t, weighted, targets, sources, ids):
        for d in range(4):

            @pl.when(sources[d])
            def _():
                halo_copy(turn, d, ids).wait_recv()

            @pl.when(jnp.logical_not(sources[d]))
            def _():
                halo_in[turn, d] = jnp.zeros((slots, width), BF)

            @pl.when(targets[d])
            def _():
                halo_copy(turn, d, ids).wait_send()

            if weighted:
                scaled = halo_in[turn, d].astype(F32) * col_w[d * slots : (d + 1) * slots, :]
                halo_in[turn, d] = scaled.astype(BF)

        @pl.loop(0, nodes // 256)
        def _(i):
            at = pl.ds(pl.multiple_of(i * 256, 256), 256)
            acc[at, :] += mm(hot_t[at, :], halo_in[turn].reshape(4 * slots, width))

    def local_part(matrix, source):
        @pl.loop(0, nodes // 256)
        def _(i):
            at = pl.ds(pl.multiple_of(i * 256, 256), 256)
            acc[at, :] = mm(matrix[at, :], source[...])

    halo_send(0, feat, send_hot, False, ahead, ahead_id)

    @pl.loop(0, blocks)
    def _(r):
        values = [adj[r, k].astype(F32) for k in range(tiles)]
        turned = [v.T for v in values]
        across = pl.ds(pl.multiple_of(r * tb, tb), tb)
        for c in range(blocks):
            gates = [jnp.where(colb[r, k] == c, 1.0, 0.0).astype(F32) for k in range(tiles)]
            dense[across, c * tb : (c + 1) * tb] = sum(v * g for v, g in zip(values, gates)).astype(BF)
            dense_t[c * tb : (c + 1) * tb, across] = sum(v * g for v, g in zip(turned, gates)).astype(BF)

    local_part(dense, feat)
    build_cols(recv_hot_t, 1)
    halo_take(0, recv_hot_t, True, ahead, behind, ahead_id)

    def up(s, c):
        at = pl.ds(c * step, step)
        return remote(
            gathered.at[s, at], gathered.at[s, at], up_ss.at[s, c], ag_rs.at[s, c], (ix, iy, z + 1)
        )

    def down(s, c):
        at = pl.ds(c * step, step)
        return remote(
            gathered.at[s, at], gathered.at[s, at], down_ss.at[s, c], ag_rs.at[s, c], (ix, iy, z - 1)
        )

    for c in range(CHUNKS):
        gathered[z, c * step : (c + 1) * step] = acc[c * step : (c + 1) * step].astype(BF)

        @pl.when(z + 1 < af)
        def _():
            up(z, c).start()

        @pl.when(z > 0)
        def _():
            down(z, c).start()

    for k in range(1, af):
        here = lax.rem(z - k + af, af)
        remote(w_cols.at[here], w_cols.at[here], w_ss.at[k], w_rs.at[k], (ix, iy, here)).wait_recv()
    for c in range(CHUNKS):
        at = slice(c * step, (c + 1) * step)
        pre[at, :] = mm(gathered[z, at], w_cols[z])
    build_cols(send_hot_t, 0)
    build_rows(recv_hot, 1)
    for k in range(1, af):
        for c in range(CHUNKS):
            at = slice(c * step, (c + 1) * step)

            @pl.when(z - k >= 0)
            def _():
                up(z - k, c).wait_recv()

                @pl.when(z + 1 < af)
                def _():
                    up(z - k, c).start()

                pre[at, :] += mm(gathered[z - k, at], w_cols[z - k])

            @pl.when(z + k < af)
            def _():
                down(z + k, c).wait_recv()

                @pl.when(z > 0)
                def _():
                    down(z + k, c).start()

                pre[at, :] += mm(gathered[z + k, at], w_cols[z + k])

    @pl.loop(0, nodes // 64)
    def _(i):
        at = pl.ds(pl.multiple_of(i * 64, 64), 64)
        v = pre[at, :]
        field[at, :] = (v * jax.nn.sigmoid(v)).astype(BF)

    halo_send(1, field, send_hot, False, ahead, ahead_id)
    local_part(dense, field)
    halo_take(1, recv_hot_t, True, ahead, behind, ahead_id)
    mixed_hidden[...] = acc[...].astype(BF)
    for j in range(af):
        at = slice(j * quarter, (j + 1) * quarter)
        logit_out[j] = mm(mixed_hidden[at, :], wc[...]).astype(BF)
    for k in range(1, af):
        there = af_peer(k)
        remote(
            logit_out.at[there], logit_in.at[k], lo_ss.at[k], lo_rs.at[k], (ix, iy, there)
        ).start()
    mine = pl.ds(pl.multiple_of(z * quarter, quarter), quarter)
    logits = mm(mixed_hidden[mine, :], wc[...])
    for k in range(1, af):
        remote(logit_out.at[z], logit_in.at[k], lo_ss.at[k], lo_rs.at[k], (ix, iy, af_peer(k))).wait()
        logits = logits + logit_in[k].astype(F32)
    exponent = jnp.exp(logits - jnp.max(logits, axis=1, keepdims=True))
    probability = exponent / jnp.sum(exponent, axis=1, keepdims=True)
    lane = lax.broadcasted_iota(jnp.int32, (quarter, classes), 1)
    onehot = jnp.where(lane == labels[mine, :], 1.0, 0.0)
    grad_logits[z] = ((probability - onehot) * (1.0 / 64.0)).astype(BF)
    for k in range(1, af):
        remote(
            grad_logits.at[z], grad_logits.at[z], gl_ss.at[k], gl_rs.at[k], (ix, iy, af_peer(k))
        ).start()
    for k in range(1, af):
        here = lax.rem(z - k + af, af)
        remote(
            grad_logits.at[here], grad_logits.at[here], gl_ss.at[k], gl_rs.at[k], (ix, iy, here)
        ).wait_recv()
    for j in range(af):
        field[j * quarter : (j + 1) * quarter, :] = mm_nt(grad_logits[j], wc[...]).astype(BF)

    halo_send(2, field, recv_hot, True, behind, behind_id)
    class_term = mm_tn(mixed_hidden[...], grad_logits[...].reshape(nodes, classes))
    class_out[...] = class_term.astype(BF).reshape(parts, rows, classes)
    for k in range(1, parts):
        px, py = plane_peer(k)
        remote(
            class_out.at[px * gy + py], class_in.at[k], cr_ss.at[k], cr_rs.at[k], (px, py, z)
        ).start()
    local_part(dense_t, field)
    halo_take(2, send_hot_t, False, behind, ahead, behind_id)

    @pl.loop(0, nodes // 64)
    def _(i):
        at = pl.ds(pl.multiple_of(i * 64, 64), 64)
        v = pre[at, :]
        sig = jax.nn.sigmoid(v)
        field[at, :] = (acc[at, :] * sig * (1.0 + v * (1.0 - sig))).astype(BF)

    for s in range(af):
        term = mm_tn(gathered[s], field[...])
        grad_out[:, s] = term.astype(BF).reshape(parts, rows, width)
    for k in range(1, parts):
        px, py = plane_peer(k)
        remote(
            grad_out.at[px * gy + py], grad_in.at[k], rs_ss.at[k], rs_rs.at[k], (px, py, z)
        ).start()
    class_sum = class_out[me].astype(F32)
    for k in range(1, parts):
        px, py = plane_peer(k)
        remote(class_out.at[me], class_in.at[k], cr_ss.at[k], cr_rs.at[k], (px, py, z)).wait()
        class_sum = class_sum + class_in[k].astype(F32)
    whole_c[me] = class_sum.astype(BF)
    for k in range(1, parts):
        px, py = plane_peer(k)
        remote(whole_c.at[me], whole_c.at[me], fc_ss.at[k], fc_rs.at[k], (px, py, z)).start()
    for k in range(1, parts):
        px, py = plane_peer(k)
        remote(grad_out.at[me], grad_in.at[k], rs_ss.at[k], rs_rs.at[k], (px, py, z)).wait()
    for s in range(af):
        total = grad_out[me, s].astype(F32)
        for k in range(1, parts):
            total = total + grad_in[k, s].astype(F32)
        piece_out[s] = total.astype(BF)
    for k in range(1, af):
        there = af_peer(k)
        remote(
            piece_out.at[there], piece_in.at[z], za_ss.at[k], za_rs.at[k], (ix, iy, there)
        ).start()
    piece_in[z] = piece_out[z]
    for k in range(1, af):
        here = lax.rem(z - k + af, af)
        remote(piece_in.at[here], piece_in.at[here], za_ss.at[k], za_rs.at[k], (ix, iy, here)).wait_recv()
    for s in range(af):
        whole_w[me, s] = piece_in[s]
    for k in range(1, parts):
        px, py = plane_peer(k)
        remote(whole_w.at[me], whole_w.at[me], fw_ss.at[k], fw_rs.at[k], (px, py, z)).start()

    for k in range(1, af):
        remote(w_cols.at[z], w_cols.at[z], w_ss.at[k], w_rs.at[k], (ix, iy, af_peer(k))).wait_send()
        remote(
            grad_logits.at[z], grad_logits.at[z], gl_ss.at[k], gl_rs.at[k], (ix, iy, af_peer(k))
        ).wait_send()
        remote(piece_out.at[z], piece_in.at[z], za_ss.at[k], za_rs.at[k], (ix, iy, af_peer(k))).wait_send()
    for s in range(af):
        for c in range(CHUNKS):

            @pl.when(jnp.logical_and(s <= z, z + 1 < af))
            def _():
                up(s, c).wait_send()

            @pl.when(jnp.logical_and(s >= z, z > 0))
            def _():
                down(s, c).wait_send()

    for k in range(1, parts):
        px = lax.rem(ix - k // gy + gx, gx)
        py = lax.rem(iy - k % gy + gy, gy)
        slot = px * gy + py
        remote(whole_c.at[slot], whole_c.at[slot], fc_ss.at[k], fc_rs.at[k], (px, py, z)).wait()
        remote(whole_w.at[slot], whole_w.at[slot], fw_ss.at[k], fw_rs.at[k], (px, py, z)).wait()
    out_c[...] = whole_c[...]
    for s in range(af):
        out_w[:, :, s * width : (s + 1) * width] = whole_w[:, s]


def local(
    sizes,
    features,
    adj_tiles,
    col_block,
    send_rows,
    send_counts,
    recv_target,
    edge_weight,
    labels,
    w_hidden,
    w_classes,
):
    gx, gy, af = sizes
    parts = gx * gy
    nodes, width = features.shape
    slots = send_rows.shape[1]
    classes = w_classes.shape[1]
    rows = width // parts
    live = jnp.arange(slots, dtype=jnp.int32)[None, :] < send_counts[:, None]
    both = jnp.stack([jnp.where(live, send_rows, -1).reshape(-1), recv_target.reshape(-1)])
    vmem = pl.BlockSpec(memory_space=pltpu.VMEM)
    smem = pl.BlockSpec(memory_space=pltpu.SMEM)
    dma = pltpu.SemaphoreType.DMA
    grad_w, grad_c = pl.pallas_call(
        functools.partial(kernel, sizes),
        out_shape=(
            jax.ShapeDtypeStruct((parts, rows, af * width), BF),
            jax.ShapeDtypeStruct((parts, rows, classes), BF),
        ),
        in_specs=[vmem, vmem, smem, vmem, vmem, vmem, vmem, vmem, vmem],
        out_specs=(vmem, vmem),
        scratch_shapes=[
            pltpu.VMEM((4 * slots, nodes), BF),
            pltpu.VMEM((nodes, 4 * slots), BF),
            pltpu.VMEM((4 * slots, nodes), BF),
            pltpu.VMEM((nodes, 4 * slots), BF),
            pltpu.VMEM((nodes, nodes), BF),
            pltpu.VMEM((nodes, nodes), BF),
            pltpu.VMEM((nodes, width), F32),
            pltpu.VMEM((nodes, width), BF),
            pltpu.VMEM((3, 4, slots, width), BF),
            pltpu.VMEM((3, 4, slots, width), BF),
            pltpu.VMEM((af, nodes, width), BF),
            pltpu.VMEM((af, width, width), BF),
            pltpu.VMEM((nodes, width), F32),
            pltpu.VMEM((nodes, width), BF),
            pltpu.VMEM((af, nodes // af, classes), BF),
            pltpu.VMEM((af, nodes // af, classes), BF),
            pltpu.VMEM((af, nodes // af, classes), BF),
            pltpu.VMEM((parts, af, rows, width), BF),
            pltpu.VMEM((parts, af, rows, width), BF),
            pltpu.VMEM((parts, rows, classes), BF),
            pltpu.VMEM((parts, rows, classes), BF),
            pltpu.VMEM((af, rows, width), BF),
            pltpu.VMEM((af, rows, width), BF),
            pltpu.VMEM((parts, af, rows, width), BF),
            pltpu.VMEM((parts, rows, classes), BF),
            dma((3, 4)),
            dma((3, 4)),
            dma((af, CHUNKS)),
            dma((af, CHUNKS)),
            dma((af, CHUNKS)),
            dma((af,)),
            dma((af,)),
            dma((af,)),
            dma((af,)),
            dma((af,)),
            dma((af,)),
            dma((parts,)),
            dma((parts,)),
            dma((parts,)),
            dma((parts,)),
            dma((af,)),
            dma((af,)),
            dma((parts,)),
            dma((parts,)),
            dma((parts,)),
            dma((parts,)),
        ],
        compiler_params=pltpu.CompilerParams(
            collective_id=0, has_side_effects=True, vmem_limit_bytes=56 * 1024 * 1024
        ),
        name="gcn_step",
    )(
        features,
        adj_tiles,
        col_block,
        both,
        both.T,
        edge_weight.reshape(-1, 1),
        labels.reshape(-1, 1),
        w_hidden,
        w_classes,
    )
    return (
        grad_w.reshape(width, af * width).astype(F32),
        grad_c.reshape(width, classes).astype(F32),
    )


def solution(mesh):
    sizes = (mesh.shape["gx"], mesh.shape["gy"], mesh.shape["af"])
    placed = (
        P(("gx", "gy"), "af"),
        P(("gx", "gy"), None, None, None),
        P(("gx", "gy"), None),
        P(("gx", "gy"), None),
        P(("gx", "gy")),
        P(("gx", "gy"), None),
        P(("gx", "gy"), None),
        P(("gx", "gy")),
        P("af", None),
        P("af", None),
    )
    return jax.shard_map(
        functools.partial(local, sizes),
        mesh=mesh,
        in_specs=placed,
        out_specs=(P("af", None), P("af", None)),
        check_vma=False,
    )
```

```python
import functools

import jax
import jax.numpy as jnp
from jax import lax
from jax.experimental import pallas as pl
from jax.experimental.pallas import tpu as pltpu
from jax.sharding import PartitionSpec as P

MESH = pl.DeviceIdType.MESH
BF = jnp.bfloat16
F32 = jnp.float32
CHUNKS = 4


def mm(a, b):
    return jnp.dot(a, b, preferred_element_type=F32)


def mm_tn(a, b):
    return lax.dot_general(a, b, (((0,), (0,)), ((), ())), preferred_element_type=F32)


def mm_nt(a, b):
    return lax.dot_general(a, b, (((1,), (1,)), ((), ())), preferred_element_type=F32)


def kernel(
    sizes,
    feat,
    adj,
    colb,
    send_rows,
    counts,
    recv_rows,
    weights,
    labels,
    wh,
    wc,
    out_w,
    out_c,
    send_hot,
    send_hot_t,
    recv_hot,
    recv_hot_t,
    columns,
    scales,
    dense,
    dense_t,
    acc,
    field,
    halo_out,
    halo_in,
    halo_low,
    gathered,
    w_cols,
    pre,
    mixed_hidden,
    logit_out,
    logit_in,
    grad_logits,
    grad_out,
    grad_in,
    class_out,
    class_in,
    piece_out,
    whole_w,
    whole_c,
    halo_ss,
    halo_rs,
    up_ss,
    down_ss,
    ag_rs,
    w_ss,
    w_rs,
    lo_ss,
    lo_rs,
    gl_ss,
    gl_rs,
    rs_ss,
    rs_rs,
    cr_ss,
    cr_rs,
    za_ss,
    za_rs,
    fw_ss,
    fw_rs,
    fc_ss,
    fc_rs,
):
    gx, gy, af = sizes
    nodes, width = feat.shape
    slots = send_rows.shape[1]
    parts = gx * gy
    rows = width // parts
    quarter = nodes // af
    step = nodes // CHUNKS
    classes = wc.shape[1]
    blocks, tiles, tb, _ = adj.shape
    ix, iy, z = lax.axis_index("gx"), lax.axis_index("gy"), lax.axis_index("af")
    me = ix * gy + iy

    def plane_peer(k):
        px = lax.rem(ix + k // gy, gx)
        py = lax.rem(iy + k % gy, gy)
        return px, py

    def af_peer(k):
        return lax.rem(z + k, af)

    def remote(src, dst, ss, rs, where):
        return pltpu.make_async_remote_copy(
            src_ref=src, dst_ref=dst, send_sem=ss, recv_sem=rs, device_id=where, device_id_type=MESH
        )

    barrier = pltpu.get_barrier_semaphore()
    for k in range(1, parts):
        px, py = plane_peer(k)
        pl.semaphore_signal(barrier, inc=1, device_id=(px, py, z), device_id_type=MESH)
    for k in range(1, af):
        pl.semaphore_signal(barrier, inc=1, device_id=(ix, iy, af_peer(k)), device_id_type=MESH)

    lane = lax.broadcasted_iota(jnp.int32, (1, slots), 1)
    live = [jnp.where(lane < counts[d], send_rows[d : d + 1, :], -1) for d in range(4)]
    taken = [recv_rows[d : d + 1, :] for d in range(4)]
    columns[...] = jnp.concatenate([v.astype(F32) for v in live + taken], axis=0).T
    scales[...] = jnp.concatenate([weights[...], weights[...]], axis=0).T

    def build_rows(hot, first):
        for d in range(4):

            @pl.loop(0, slots // 32)
            def _(i):
                at = pl.multiple_of(i * 32, 32)
                ids = columns[pl.ds(at, 32), first + d : first + d + 1].astype(jnp.int32)
                node = lax.broadcasted_iota(jnp.int32, (32, nodes), 1)
                hot[pl.ds(at + d * slots, 32), :] = jnp.where(node == ids, 1.0, 0.0).astype(BF)

    def build_cols(hot, rows_of):
        @pl.loop(0, nodes // 32)
        def _(i):
            at = pl.ds(pl.multiple_of(i * 32, 32), 32)
            node = lax.broadcasted_iota(jnp.int32, (32, slots), 0) + i * 32
            for d in range(4):
                hot[at, d * slots : (d + 1) * slots] = jnp.where(node == rows_of[d], 1.0, 0.0).astype(BF)

    build_rows(send_hot, 0)
    pl.semaphore_wait(barrier, parts - 1 + af - 1)

    for k in range(1, af):
        there = af_peer(k)
        remote(
            wh.at[:, pl.ds(pl.multiple_of(there * width, width), width)],
            w_cols.at[z],
            w_ss.at[k],
            w_rs.at[k],
            (ix, iy, there),
        ).start()
    w_cols[z] = wh[:, pl.ds(pl.multiple_of(z * width, width), width)]

    ahead = ((ix + 1 < gx), (ix > 0), (iy + 1 < gy), (iy > 0))
    behind = ((ix > 0), (ix + 1 < gx), (iy > 0), (iy + 1 < gy))
    ahead_id = ((ix + 1, iy, z), (ix - 1, iy, z), (ix, iy + 1, z), (ix, iy - 1, z))
    behind_id = ((ix - 1, iy, z), (ix + 1, iy, z), (ix, iy - 1, z), (ix, iy + 1, z))

    def halo_copy(turn, d, ids):
        return remote(
            halo_out.at[turn, d], halo_in.at[turn, d], halo_ss.at[turn, d], halo_rs.at[turn, d], ids[d]
        )

    def halo_send(turn, source, hot, weighted, targets, ids):
        for d in (2, 3, 0, 1):
            picked = mm(hot[d * slots : (d + 1) * slots, :], source[...])
            if weighted:
                picked = picked * scales[:, d : d + 1]
            halo_out[turn, d] = picked.astype(BF)

            @pl.when(targets[d])
            def _():
                halo_copy(turn, d, ids).start()

    def halo_take(turn, hot_t, weighted, targets, sources, ids, finish):
        for pair in ((0, 1), (2, 3)):
            for d in pair:

                @pl.when(sources[d])
                def _():
                    halo_copy(turn, d, ids).wait_recv()

                @pl.when(jnp.logical_not(sources[d]))
                def _():
                    halo_in[turn, d] = jnp.zeros((slots, width), BF)

                if weighted:
                    scaled = halo_in[turn, d].astype(F32) * scales[:, d : d + 1]
                    high = scaled.astype(BF)
                    halo_in[turn, d] = high
                    halo_low[d] = (scaled - high.astype(F32)).astype(BF)
            first, last = pair[0] * slots, (pair[1] + 1) * slots

            def add(at):
                hot_part = hot_t[at, first:last]
                total = acc[at, :] + mm(hot_part, halo_in[turn, pair[0] : pair[1] + 1].reshape(-1, width))
                if weighted:
                    total += mm(hot_part, halo_low[pair[0] : pair[1] + 1].reshape(-1, width))
                return total

            if pair[0] == 0:

                @pl.loop(0, nodes // 256)
                def _(i):
                    at = pl.ds(pl.multiple_of(i * 256, 256), 256)
                    acc[at, :] = add(at)

            else:
                finish(add)
        for d in range(4):

            @pl.when(targets[d])
            def _():
                halo_copy(turn, d, ids).wait_send()

    def local_part(matrix, source):
        @pl.loop(0, nodes // 256)
        def _(i):
            at = pl.ds(pl.multiple_of(i * 256, 256), 256)
            acc[at, :] = mm(matrix[at, :], source[...])

    halo_send(0, feat, send_hot, False, ahead, ahead_id)

    @pl.loop(0, blocks)
    def _(r):
        values = [adj[r, k].astype(F32) for k in range(tiles)]
        turned = [v.T for v in values]
        chosen = colb[pl.ds(r, 1), :]
        across = pl.ds(pl.multiple_of(r * tb, tb), tb)
        for c in range(blocks):
            gates = [jnp.where(chosen[:, k : k + 1] == c, 1.0, 0.0) for k in range(tiles)]
            dense[across, c * tb : (c + 1) * tb] = sum(v * g for v, g in zip(values, gates)).astype(BF)
            dense_t[c * tb : (c + 1) * tb, across] = sum(v * g for v, g in zip(turned, gates)).astype(BF)

    local_part(dense, feat)
    build_cols(recv_hot_t, taken)

    def up(s, c):
        at = pl.ds(c * step, step)
        return remote(
            gathered.at[s, at], gathered.at[s, at], up_ss.at[s, c], ag_rs.at[s, c], (ix, iy, z + 1)
        )

    def down(s, c):
        at = pl.ds(c * step, step)
        return remote(
            gathered.at[s, at], gathered.at[s, at], down_ss.at[s, c], ag_rs.at[s, c], (ix, iy, z - 1)
        )

    def spread(add):
        for c in range(CHUNKS):
            gathered[z, c * step : (c + 1) * step] = add(slice(c * step, (c + 1) * step)).astype(BF)

            @pl.when(z + 1 < af)
            def _():
                up(z, c).start()

            @pl.when(z > 0)
            def _():
                down(z, c).start()

    halo_take(0, recv_hot_t, True, ahead, behind, ahead_id, spread)
    for k in range(1, af):
        here = lax.rem(z - k + af, af)
        remote(w_cols.at[here], w_cols.at[here], w_ss.at[k], w_rs.at[k], (ix, iy, here)).wait_recv()
    for c in range(CHUNKS):
        at = slice(c * step, (c + 1) * step)
        pre[at, :] = mm(gathered[z, at], w_cols[z])
    build_cols(send_hot_t, live)
    build_rows(recv_hot, 4)
    for k in range(1, af):
        for c in range(CHUNKS):
            at = slice(c * step, (c + 1) * step)

            @pl.when(z - k >= 0)
            def _():
                up(z - k, c).wait_recv()

                @pl.when(z + 1 < af)
                def _():
                    up(z - k, c).start()

                pre[at, :] += mm(gathered[z - k, at], w_cols[z - k])

            @pl.when(z + k < af)
            def _():
                down(z + k, c).wait_recv()

                @pl.when(z > 0)
                def _():
                    down(z + k, c).start()

                pre[at, :] += mm(gathered[z + k, at], w_cols[z + k])

    @pl.loop(0, nodes // 64)
    def _(i):
        at = pl.ds(pl.multiple_of(i * 64, 64), 64)
        v = pre[at, :]
        field[at, :] = (v * jax.nn.sigmoid(v)).astype(BF)

    halo_send(1, field, send_hot, False, ahead, ahead_id)
    local_part(dense, field)
    own_logits = []

    def to_classes(add):
        for k in (*range(1, af), 0):
            there = af_peer(k)
            at = pl.ds(pl.multiple_of(there * quarter, quarter), quarter)
            mixed = add(at).astype(BF)
            mixed_hidden[at, :] = mixed
            part = mm(mixed, wc[...])
            if k == 0:
                own_logits.append(part)
            else:
                logit_out[there] = part.astype(BF)
                remote(
                    logit_out.at[there], logit_in.at[k], lo_ss.at[k], lo_rs.at[k], (ix, iy, there)
                ).start()

    halo_take(1, recv_hot_t, True, ahead, behind, ahead_id, to_classes)
    logits = own_logits[0]
    for k in range(1, af):
        remote(logit_out.at[z], logit_in.at[k], lo_ss.at[k], lo_rs.at[k], (ix, iy, af_peer(k))).wait()
        logits = logits + logit_in[k].astype(F32)
    exponent = jnp.exp(logits - jnp.max(logits, axis=1, keepdims=True))
    probability = exponent / jnp.sum(exponent, axis=1, keepdims=True)
    mine = pl.ds(pl.multiple_of(z * quarter, quarter), quarter)
    kind = lax.broadcasted_iota(jnp.int32, (classes, quarter), 0)
    onehot = jnp.where(kind == labels[:, mine], 1.0, 0.0).T
    grad_logits[z] = ((probability - onehot) * (1.0 / 64.0)).astype(BF)
    for k in range(1, af):
        remote(
            grad_logits.at[z], grad_logits.at[z], gl_ss.at[k], gl_rs.at[k], (ix, iy, af_peer(k))
        ).start()
    field[mine, :] = mm_nt(grad_logits[z], wc[...]).astype(BF)
    for k in range(1, af):
        here = lax.rem(z - k + af, af)
        remote(
            grad_logits.at[here], grad_logits.at[here], gl_ss.at[k], gl_rs.at[k], (ix, iy, here)
        ).wait_recv()
        at = pl.ds(pl.multiple_of(here * quarter, quarter), quarter)
        field[at, :] = mm_nt(grad_logits[here], wc[...]).astype(BF)

    halo_send(2, field, recv_hot, True, behind, behind_id)
    class_term = mm_tn(mixed_hidden[...], grad_logits[...].reshape(nodes, classes))
    class_out[...] = class_term.astype(BF).reshape(parts, rows, classes)
    for k in range(1, parts):
        px, py = plane_peer(k)
        remote(
            class_out.at[px * gy + py], class_in.at[k], cr_ss.at[k], cr_rs.at[k], (px, py, z)
        ).start()
    local_part(dense_t, field)
    def to_grad_pre(add):
        @pl.loop(0, nodes // 128)
        def _(i):
            at = pl.ds(pl.multiple_of(i * 128, 128), 128)
            v = pre[at, :]
            sig = jax.nn.sigmoid(v)
            field[at, :] = (add(at) * sig * (1.0 + v * (1.0 - sig))).astype(BF)

    halo_take(2, send_hot_t, False, behind, ahead, behind_id, to_grad_pre)

    def piece(k, j, slot):
        px, py = plane_peer(j)
        return remote(
            grad_out.at[k, slot], grad_in.at[k, j], rs_ss.at[k, j], rs_rs.at[k, j], (px, py, z)
        )

    order = (*range(1, af), 0)
    for k in order:
        term = mm_tn(gathered[af_peer(k)], field[...])
        grad_out[k] = term.astype(BF).reshape(parts, rows, width)
        for j in range(1, parts):
            px, py = plane_peer(j)
            piece(k, j, px * gy + py).start()
    class_sum = class_out[me].astype(F32)
    for k in range(1, parts):
        px, py = plane_peer(k)
        remote(class_out.at[me], class_in.at[k], cr_ss.at[k], cr_rs.at[k], (px, py, z)).wait()
        class_sum = class_sum + class_in[k].astype(F32)
    whole_c[me] = class_sum.astype(BF)
    for k in range(1, parts):
        px, py = plane_peer(k)
        remote(whole_c.at[me], whole_c.at[me], fc_ss.at[k], fc_rs.at[k], (px, py, z)).start()
    for k in order:
        total = grad_out[k, me].astype(F32)
        for j in range(1, parts):
            piece(k, j, me).wait()
            total = total + grad_in[k, j].astype(F32)
        piece_out[k] = total.astype(BF)
        if k > 0:
            remote(
                piece_out.at[k], whole_w.at[me, z], za_ss.at[k], za_rs.at[k], (ix, iy, af_peer(k))
            ).start()

    def share(k, j, slot, s, where):
        return remote(
            whole_w.at[slot, s], whole_w.at[slot, s], fw_ss.at[k, j], fw_rs.at[k, j], (*where, z)
        )

    whole_w[me, z] = piece_out[0]
    for k in range(af):
        here = lax.rem(z - k + af, af)
        if k > 0:
            remote(
                piece_out.at[k], whole_w.at[me, here], za_ss.at[k], za_rs.at[k], (ix, iy, here)
            ).wait_recv()
        for j in range(1, parts):
            share(k, j, me, here, plane_peer(j)).start()

    for k in range(1, af):
        remote(w_cols.at[z], w_cols.at[z], w_ss.at[k], w_rs.at[k], (ix, iy, af_peer(k))).wait_send()
        remote(
            grad_logits.at[z], grad_logits.at[z], gl_ss.at[k], gl_rs.at[k], (ix, iy, af_peer(k))
        ).wait_send()
        remote(piece_out.at[k], whole_w.at[me, z], za_ss.at[k], za_rs.at[k], (ix, iy, af_peer(k))).wait_send()
    for s in range(af):
        for c in range(CHUNKS):

            @pl.when(jnp.logical_and(s <= z, z + 1 < af))
            def _():
                up(s, c).wait_send()

            @pl.when(jnp.logical_and(s >= z, z > 0))
            def _():
                down(s, c).wait_send()

    for k in range(1, parts):
        px = lax.rem(ix - k // gy + gx, gx)
        py = lax.rem(iy - k % gy + gy, gy)
        slot = px * gy + py
        remote(whole_c.at[slot], whole_c.at[slot], fc_ss.at[k], fc_rs.at[k], (px, py, z)).wait()
        for m in range(af):
            share(m, k, slot, lax.rem(z - m + af, af), (px, py)).wait()
    out_c[...] = whole_c[...]
    for s in range(af):
        out_w[:, :, s * width : (s + 1) * width] = whole_w[:, s]


def local(
    sizes,
    features,
    adj_tiles,
    col_block,
    send_rows,
    send_counts,
    recv_target,
    edge_weight,
    labels,
    w_hidden,
    w_classes,
):
    gx, gy, af = sizes
    parts = gx * gy
    nodes, width = features.shape
    slots = send_rows.shape[1]
    classes = w_classes.shape[1]
    rows = width // parts
    vmem = pl.BlockSpec(memory_space=pltpu.VMEM)
    smem = pl.BlockSpec(memory_space=pltpu.SMEM)
    dma = pltpu.SemaphoreType.DMA
    grad_w, grad_c = pl.pallas_call(
        functools.partial(kernel, sizes),
        out_shape=(
            jax.ShapeDtypeStruct((parts, rows, af * width), BF),
            jax.ShapeDtypeStruct((parts, rows, classes), BF),
        ),
        in_specs=[vmem, vmem, vmem, vmem, smem, vmem, vmem, vmem, vmem, vmem],
        out_specs=(vmem, vmem),
        scratch_shapes=[
            pltpu.VMEM((4 * slots, nodes), BF),
            pltpu.VMEM((nodes, 4 * slots), BF),
            pltpu.VMEM((4 * slots, nodes), BF),
            pltpu.VMEM((nodes, 4 * slots), BF),
            pltpu.VMEM((slots, 8), F32),
            pltpu.VMEM((slots, 8), F32),
            pltpu.VMEM((nodes, nodes), BF),
            pltpu.VMEM((nodes, nodes), BF),
            pltpu.VMEM((nodes, width), F32),
            pltpu.VMEM((nodes, width), BF),
            pltpu.VMEM((3, 4, slots, width), BF),
            pltpu.VMEM((3, 4, slots, width), BF),
            pltpu.VMEM((4, slots, width), BF),
            pltpu.VMEM((af, nodes, width), BF),
            pltpu.VMEM((af, width, width), BF),
            pltpu.VMEM((nodes, width), F32),
            pltpu.VMEM((nodes, width), BF),
            pltpu.VMEM((af, nodes // af, classes), BF),
            pltpu.VMEM((af, nodes // af, classes), BF),
            pltpu.VMEM((af, nodes // af, classes), BF),
            pltpu.VMEM((af, parts, rows, width), BF),
            pltpu.VMEM((af, parts, rows, width), BF),
            pltpu.VMEM((parts, rows, classes), BF),
            pltpu.VMEM((parts, rows, classes), BF),
            pltpu.VMEM((af, rows, width), BF),
            pltpu.VMEM((parts, af, rows, width), BF),
            pltpu.VMEM((parts, rows, classes), BF),
            dma((3, 4)),
            dma((3, 4)),
            dma((af, CHUNKS)),
            dma((af, CHUNKS)),
            dma((af, CHUNKS)),
            dma((af,)),
            dma((af,)),
            dma((af,)),
            dma((af,)),
            dma((af,)),
            dma((af,)),
            dma((af, parts)),
            dma((af, parts)),
            dma((parts,)),
            dma((parts,)),
            dma((af,)),
            dma((af,)),
            dma((af, parts)),
            dma((af, parts)),
            dma((parts,)),
            dma((parts,)),
        ],
        compiler_params=pltpu.CompilerParams(
            collective_id=0, has_side_effects=True, vmem_limit_bytes=56 * 1024 * 1024
        ),
        name="gcn_step",
    )(
        features,
        adj_tiles,
        col_block,
        send_rows,
        send_counts,
        recv_target,
        edge_weight,
        labels.reshape(1, -1),
        w_hidden,
        w_classes,
    )
    return (
        grad_w.reshape(width, af * width).astype(F32),
        grad_c.reshape(width, classes).astype(F32),
    )


def solution(mesh):
    sizes = (mesh.shape["gx"], mesh.shape["gy"], mesh.shape["af"])
    placed = (
        P(("gx", "gy"), "af"),
        P(("gx", "gy"), None, None, None),
        P(("gx", "gy"), None),
        P(("gx", "gy"), None),
        P(("gx", "gy")),
        P(("gx", "gy"), None),
        P(("gx", "gy"), None),
        P(("gx", "gy")),
        P("af", None),
        P("af", None),
    )
    return jax.shard_map(
        functools.partial(local, sizes),
        mesh=mesh,
        in_specs=placed,
        out_specs=(P("af", None), P("af", None)),
        check_vma=False,
    )
```

```python
import functools

import jax
import jax.numpy as jnp
from jax import lax
from jax.experimental import pallas as pl
from jax.experimental.pallas import tpu as pltpu
from jax.sharding import PartitionSpec as P

MESH = pl.DeviceIdType.MESH
BF = jnp.bfloat16
F32 = jnp.float32
CHUNKS = 4


def mm(a, b):
    return jnp.dot(a, b, preferred_element_type=F32)


def mm_tn(a, b):
    return lax.dot_general(a, b, (((0,), (0,)), ((), ())), preferred_element_type=F32)


def mm_nt(a, b):
    return lax.dot_general(a, b, (((1,), (1,)), ((), ())), preferred_element_type=F32)


def kernel(
    sizes,
    feat,
    adj,
    colb,
    send_rows,
    counts,
    recv_rows,
    weights,
    labels,
    wh,
    wc,
    out_w,
    out_c,
    send_hot,
    send_hot_t,
    recv_hot,
    recv_hot_t,
    columns,
    scales,
    dense,
    dense_t,
    acc,
    field,
    halo_out,
    halo_in,
    halo_low,
    gathered,
    gathered_t,
    w_cols,
    pre,
    mixed_hidden,
    logit_out,
    logit_in,
    grad_logits,
    grad_out,
    grad_in,
    class_out,
    class_in,
    piece_out,
    whole_w,
    whole_c,
    halo_ss,
    halo_rs,
    up_ss,
    down_ss,
    ag_rs,
    w_ss,
    w_rs,
    lo_ss,
    lo_rs,
    gl_ss,
    gl_rs,
    rs_ss,
    rs_rs,
    cr_ss,
    cr_rs,
    za_ss,
    za_rs,
    fw_ss,
    fw_rs,
    fc_ss,
    fc_rs,
):
    gx, gy, af = sizes
    nodes, width = feat.shape
    slots = send_rows.shape[1]
    parts = gx * gy
    rows = width // parts
    quarter = nodes // af
    step = nodes // CHUNKS
    classes = wc.shape[1]
    blocks, tiles, tb, _ = adj.shape
    ix, iy, z = lax.axis_index("gx"), lax.axis_index("gy"), lax.axis_index("af")
    me = ix * gy + iy

    def plane_peer(k):
        px = lax.rem(ix + k // gy, gx)
        py = lax.rem(iy + k % gy, gy)
        return px, py

    def af_peer(k):
        return lax.rem(z + k, af)

    def remote(src, dst, ss, rs, where):
        return pltpu.make_async_remote_copy(
            src_ref=src, dst_ref=dst, send_sem=ss, recv_sem=rs, device_id=where, device_id_type=MESH
        )

    barrier = pltpu.get_barrier_semaphore()
    for k in range(1, parts):
        px, py = plane_peer(k)
        pl.semaphore_signal(barrier, inc=1, device_id=(px, py, z), device_id_type=MESH)
    for k in range(1, af):
        pl.semaphore_signal(barrier, inc=1, device_id=(ix, iy, af_peer(k)), device_id_type=MESH)

    lane = lax.broadcasted_iota(jnp.int32, (1, slots), 1)
    live = [jnp.where(lane < counts[d], send_rows[d : d + 1, :], -1) for d in range(4)]
    taken = [recv_rows[d : d + 1, :] for d in range(4)]
    columns[...] = jnp.concatenate([v.astype(F32) for v in live + taken], axis=0).T
    scales[...] = jnp.concatenate([weights[...], weights[...]], axis=0).T

    def build_rows(hot, first):
        for d in range(4):

            @pl.loop(0, slots // 32)
            def _(i):
                at = pl.multiple_of(i * 32, 32)
                ids = columns[pl.ds(at, 32), first + d : first + d + 1].astype(jnp.int32)
                node = lax.broadcasted_iota(jnp.int32, (32, nodes), 1)
                hot[pl.ds(at + d * slots, 32), :] = jnp.where(node == ids, 1.0, 0.0).astype(BF)

    def build_cols(hot, rows_of):
        @pl.loop(0, nodes // 32)
        def _(i):
            at = pl.ds(pl.multiple_of(i * 32, 32), 32)
            node = lax.broadcasted_iota(jnp.int32, (32, slots), 0) + i * 32
            for d in range(4):
                hot[at, d * slots : (d + 1) * slots] = jnp.where(node == rows_of[d], 1.0, 0.0).astype(BF)

    build_rows(send_hot, 0)
    pl.semaphore_wait(barrier, parts - 1 + af - 1)

    for k in range(1, af):
        there = af_peer(k)
        remote(
            wh.at[:, pl.ds(pl.multiple_of(there * width, width), width)],
            w_cols.at[z],
            w_ss.at[k],
            w_rs.at[k],
            (ix, iy, there),
        ).start()
    w_cols[z] = wh[:, pl.ds(pl.multiple_of(z * width, width), width)]

    ahead = ((ix + 1 < gx), (ix > 0), (iy + 1 < gy), (iy > 0))
    behind = ((ix > 0), (ix + 1 < gx), (iy > 0), (iy + 1 < gy))
    ahead_id = ((ix + 1, iy, z), (ix - 1, iy, z), (ix, iy + 1, z), (ix, iy - 1, z))
    behind_id = ((ix - 1, iy, z), (ix + 1, iy, z), (ix, iy - 1, z), (ix, iy + 1, z))

    def halo_copy(turn, d, ids):
        return remote(
            halo_out.at[turn, d], halo_in.at[turn, d], halo_ss.at[turn, d], halo_rs.at[turn, d], ids[d]
        )

    def halo_send(turn, source, hot, weighted, targets, ids):
        for d in (2, 3, 0, 1):
            picked = mm(hot[d * slots : (d + 1) * slots, :], source[...])
            if weighted:
                picked = picked * scales[:, d : d + 1]
            halo_out[turn, d] = picked.astype(BF)

            @pl.when(targets[d])
            def _():
                halo_copy(turn, d, ids).start()

    def halo_take(turn, hot_t, weighted, targets, sources, ids, finish):
        for pair in ((0, 1), (2, 3)):
            for d in pair:

                @pl.when(sources[d])
                def _():
                    halo_copy(turn, d, ids).wait_recv()

                @pl.when(jnp.logical_not(sources[d]))
                def _():
                    halo_in[turn, d] = jnp.zeros((slots, width), BF)

                if weighted:
                    scaled = halo_in[turn, d].astype(F32) * scales[:, d : d + 1]
                    high = scaled.astype(BF)
                    halo_in[turn, d] = high
                    halo_low[d] = (scaled - high.astype(F32)).astype(BF)
            first, last = pair[0] * slots, (pair[1] + 1) * slots

            def add(at):
                hot_part = hot_t[at, first:last]
                total = acc[at, :] + mm(hot_part, halo_in[turn, pair[0] : pair[1] + 1].reshape(-1, width))
                if weighted:
                    total += mm(hot_part, halo_low[pair[0] : pair[1] + 1].reshape(-1, width))
                return total

            if pair[0] == 0:

                @pl.loop(0, nodes // 256)
                def _(i):
                    at = pl.ds(pl.multiple_of(i * 256, 256), 256)
                    acc[at, :] = add(at)

            else:
                finish(add)
        for d in range(4):

            @pl.when(targets[d])
            def _():
                halo_copy(turn, d, ids).wait_send()

    def local_part(matrix, source):
        @pl.loop(0, nodes // 256)
        def _(i):
            at = pl.ds(pl.multiple_of(i * 256, 256), 256)
            acc[at, :] = mm(matrix[at, :], source[...])

    halo_send(0, feat, send_hot, False, ahead, ahead_id)

    def gates(r, c):
        lane_r = lax.broadcasted_iota(jnp.int32, (tiles, blocks), 1) == r
        chosen = jnp.sum(jnp.where(lane_r, colb[...].astype(F32), 0.0), axis=1, keepdims=True)
        return [jnp.where(chosen[k : k + 1, :] == c, 1.0, 0.0) for k in range(tiles)]

    @pl.loop(0, blocks)
    def _(r):
        values = [adj[r, k].astype(F32) for k in range(tiles)]
        across = pl.ds(pl.multiple_of(r * tb, tb), tb)
        for c in range(blocks):
            tile = sum(v * g for v, g in zip(values, gates(r, c)))
            dense[across, c * tb : (c + 1) * tb] = tile.astype(BF)

    local_part(dense, feat)
    build_cols(recv_hot_t, taken)

    def up(s, c):
        at = pl.ds(c * step, step)
        return remote(
            gathered.at[s, at], gathered.at[s, at], up_ss.at[s, c], ag_rs.at[s, c], (ix, iy, z + 1)
        )

    def down(s, c):
        at = pl.ds(c * step, step)
        return remote(
            gathered.at[s, at], gathered.at[s, at], down_ss.at[s, c], ag_rs.at[s, c], (ix, iy, z - 1)
        )

    def spread(add):
        for c in range(CHUNKS):
            gathered[z, c * step : (c + 1) * step] = add(slice(c * step, (c + 1) * step)).astype(BF)

            @pl.when(z + 1 < af)
            def _():
                up(z, c).start()

            @pl.when(z > 0)
            def _():
                down(z, c).start()

    halo_take(0, recv_hot_t, True, ahead, behind, ahead_id, spread)
    for k in range(1, af):
        here = lax.rem(z - k + af, af)
        remote(w_cols.at[here], w_cols.at[here], w_ss.at[k], w_rs.at[k], (ix, iy, here)).wait_recv()
    for c in range(CHUNKS):
        at = slice(c * step, (c + 1) * step)
        pre[at, :] = mm(gathered[z, at], w_cols[z])
    build_cols(send_hot_t, live)

    @pl.loop(0, blocks)
    def _(r):
        turned = [adj[r, k].astype(F32).T for k in range(tiles)]
        across = pl.ds(pl.multiple_of(r * tb, tb), tb)
        for c in range(blocks):
            tile = sum(v * g for v, g in zip(turned, gates(r, c)))
            dense_t[c * tb : (c + 1) * tb, across] = tile.astype(BF)

    build_rows(recv_hot, 4)
    for k in range(1, af):
        for c in range(CHUNKS):
            at = slice(c * step, (c + 1) * step)

            @pl.when(z - k >= 0)
            def _():
                up(z - k, c).wait_recv()

                @pl.when(z + 1 < af)
                def _():
                    up(z - k, c).start()

                pre[at, :] += mm(gathered[z - k, at], w_cols[z - k])

            @pl.when(z + k < af)
            def _():
                down(z + k, c).wait_recv()

                @pl.when(z > 0)
                def _():
                    down(z + k, c).start()

                pre[at, :] += mm(gathered[z + k, at], w_cols[z + k])

    @pl.loop(0, nodes // 64)
    def _(i):
        at = pl.ds(pl.multiple_of(i * 64, 64), 64)
        v = pre[at, :]
        field[at, :] = (v * jax.nn.sigmoid(v)).astype(BF)

    halo_send(1, field, send_hot, False, ahead, ahead_id)
    local_part(dense, field)
    for s in range(af):
        for i in range(nodes // 256):
            gathered_t[s, :, i * 256 : (i + 1) * 256] = gathered[s, i * 256 : (i + 1) * 256].T
    own_logits = []

    def to_classes(add):
        for k in (*range(1, af), 0):
            there = af_peer(k)
            at = pl.ds(pl.multiple_of(there * quarter, quarter), quarter)
            mixed = add(at).astype(BF)
            mixed_hidden[at, :] = mixed
            part = mm(mixed, wc[...])
            if k == 0:
                own_logits.append(part)
            else:
                logit_out[there] = part.astype(BF)
                remote(
                    logit_out.at[there], logit_in.at[k], lo_ss.at[k], lo_rs.at[k], (ix, iy, there)
                ).start()

    halo_take(1, recv_hot_t, True, ahead, behind, ahead_id, to_classes)
    logits = own_logits[0]
    for k in range(1, af):
        remote(logit_out.at[z], logit_in.at[k], lo_ss.at[k], lo_rs.at[k], (ix, iy, af_peer(k))).wait()
        logits = logits + logit_in[k].astype(F32)
    exponent = jnp.exp(logits - jnp.max(logits, axis=1, keepdims=True))
    probability = exponent / jnp.sum(exponent, axis=1, keepdims=True)
    mine = pl.ds(pl.multiple_of(z * quarter, quarter), quarter)
    kind = lax.broadcasted_iota(jnp.int32, (classes, quarter), 0)
    onehot = jnp.where(kind == labels[:, mine], 1.0, 0.0).T
    grad_logits[z] = ((probability - onehot) * (1.0 / 64.0)).astype(BF)
    for k in range(1, af):
        remote(
            grad_logits.at[z], grad_logits.at[z], gl_ss.at[k], gl_rs.at[k], (ix, iy, af_peer(k))
        ).start()
    field[mine, :] = mm_nt(grad_logits[z], wc[...]).astype(BF)
    for k in range(1, af):
        here = lax.rem(z - k + af, af)
        remote(
            grad_logits.at[here], grad_logits.at[here], gl_ss.at[k], gl_rs.at[k], (ix, iy, here)
        ).wait_recv()
        at = pl.ds(pl.multiple_of(here * quarter, quarter), quarter)
        field[at, :] = mm_nt(grad_logits[here], wc[...]).astype(BF)

    halo_send(2, field, recv_hot, True, behind, behind_id)
    class_term = mm_tn(mixed_hidden[...], grad_logits[...].reshape(nodes, classes))
    class_out[...] = class_term.astype(BF).reshape(parts, rows, classes)
    for k in range(1, parts):
        px, py = plane_peer(k)
        remote(
            class_out.at[px * gy + py], class_in.at[k], cr_ss.at[k], cr_rs.at[k], (px, py, z)
        ).start()
    local_part(dense_t, field)
    def to_grad_pre(add):
        @pl.loop(0, nodes // 128)
        def _(i):
            at = pl.ds(pl.multiple_of(i * 128, 128), 128)
            v = pre[at, :]
            sig = jax.nn.sigmoid(v)
            field[at, :] = (add(at) * sig * (1.0 + v * (1.0 - sig))).astype(BF)

    halo_take(2, send_hot_t, False, behind, ahead, behind_id, to_grad_pre)

    def piece(k, j, slot):
        px, py = plane_peer(j)
        return remote(
            grad_out.at[k, slot], grad_in.at[k, j], rs_ss.at[k, j], rs_rs.at[k, j], (px, py, z)
        )

    order = (*range(1, af), 0)
    for k in order:
        term = mm(gathered_t[af_peer(k)], field[...])
        grad_out[k] = term.astype(BF).reshape(parts, rows, width)
        for j in range(1, parts):
            px, py = plane_peer(j)
            piece(k, j, px * gy + py).start()
    class_sum = class_out[me].astype(F32)
    for k in range(1, parts):
        px, py = plane_peer(k)
        remote(class_out.at[me], class_in.at[k], cr_ss.at[k], cr_rs.at[k], (px, py, z)).wait()
        class_sum = class_sum + class_in[k].astype(F32)
    whole_c[me] = class_sum.astype(BF)
    for k in range(1, parts):
        px, py = plane_peer(k)
        remote(whole_c.at[me], whole_c.at[me], fc_ss.at[k], fc_rs.at[k], (px, py, z)).start()
    for k in order:
        total = grad_out[k, me].astype(F32)
        for j in range(1, parts):
            piece(k, j, me).wait()
            total = total + grad_in[k, j].astype(F32)
        piece_out[k] = total.astype(BF)
        if k > 0:
            remote(
                piece_out.at[k], whole_w.at[me, z], za_ss.at[k], za_rs.at[k], (ix, iy, af_peer(k))
            ).start()

    def share(k, j, slot, s, where):
        return remote(
            whole_w.at[slot, s], whole_w.at[slot, s], fw_ss.at[k, j], fw_rs.at[k, j], (*where, z)
        )

    whole_w[me, z] = piece_out[0]
    for k in range(af):
        here = lax.rem(z - k + af, af)
        if k > 0:
            remote(
                piece_out.at[k], whole_w.at[me, here], za_ss.at[k], za_rs.at[k], (ix, iy, here)
            ).wait_recv()
        for j in range(1, parts):
            share(k, j, me, here, plane_peer(j)).start()

    for k in range(1, af):
        remote(w_cols.at[z], w_cols.at[z], w_ss.at[k], w_rs.at[k], (ix, iy, af_peer(k))).wait_send()
        remote(
            grad_logits.at[z], grad_logits.at[z], gl_ss.at[k], gl_rs.at[k], (ix, iy, af_peer(k))
        ).wait_send()
        remote(piece_out.at[k], whole_w.at[me, z], za_ss.at[k], za_rs.at[k], (ix, iy, af_peer(k))).wait_send()
    for s in range(af):
        for c in range(CHUNKS):

            @pl.when(jnp.logical_and(s <= z, z + 1 < af))
            def _():
                up(s, c).wait_send()

            @pl.when(jnp.logical_and(s >= z, z > 0))
            def _():
                down(s, c).wait_send()

    for k in range(1, parts):
        px = lax.rem(ix - k // gy + gx, gx)
        py = lax.rem(iy - k % gy + gy, gy)
        slot = px * gy + py
        remote(whole_c.at[slot], whole_c.at[slot], fc_ss.at[k], fc_rs.at[k], (px, py, z)).wait()
        for m in range(af):
            share(m, k, slot, lax.rem(z - m + af, af), (px, py)).wait()
    out_c[...] = whole_c[...]
    for s in range(af):
        out_w[:, :, s * width : (s + 1) * width] = whole_w[:, s]


def local(
    sizes,
    features,
    adj_tiles,
    col_block,
    send_rows,
    send_counts,
    recv_target,
    edge_weight,
    labels,
    w_hidden,
    w_classes,
):
    gx, gy, af = sizes
    parts = gx * gy
    nodes, width = features.shape
    slots = send_rows.shape[1]
    classes = w_classes.shape[1]
    rows = width // parts
    vmem = pl.BlockSpec(memory_space=pltpu.VMEM)
    smem = pl.BlockSpec(memory_space=pltpu.SMEM)
    dma = pltpu.SemaphoreType.DMA
    grad_w, grad_c = pl.pallas_call(
        functools.partial(kernel, sizes),
        out_shape=(
            jax.ShapeDtypeStruct((parts, rows, af * width), BF),
            jax.ShapeDtypeStruct((parts, rows, classes), BF),
        ),
        in_specs=[vmem, vmem, vmem, vmem, smem, vmem, vmem, vmem, vmem, vmem],
        out_specs=(vmem, vmem),
        scratch_shapes=[
            pltpu.VMEM((4 * slots, nodes), BF),
            pltpu.VMEM((nodes, 4 * slots), BF),
            pltpu.VMEM((4 * slots, nodes), BF),
            pltpu.VMEM((nodes, 4 * slots), BF),
            pltpu.VMEM((slots, 8), F32),
            pltpu.VMEM((slots, 8), F32),
            pltpu.VMEM((nodes, nodes), BF),
            pltpu.VMEM((nodes, nodes), BF),
            pltpu.VMEM((nodes, width), F32),
            pltpu.VMEM((nodes, width), BF),
            pltpu.VMEM((3, 4, slots, width), BF),
            pltpu.VMEM((3, 4, slots, width), BF),
            pltpu.VMEM((4, slots, width), BF),
            pltpu.VMEM((af, nodes, width), BF),
            pltpu.VMEM((af, width, nodes), BF),
            pltpu.VMEM((af, width, width), BF),
            pltpu.VMEM((nodes, width), F32),
            pltpu.VMEM((nodes, width), BF),
            pltpu.VMEM((af, nodes // af, classes), BF),
            pltpu.VMEM((af, nodes // af, classes), BF),
            pltpu.VMEM((af, nodes // af, classes), BF),
            pltpu.VMEM((af, parts, rows, width), BF),
            pltpu.VMEM((af, parts, rows, width), BF),
            pltpu.VMEM((parts, rows, classes), BF),
            pltpu.VMEM((parts, rows, classes), BF),
            pltpu.VMEM((af, rows, width), BF),
            pltpu.VMEM((parts, af, rows, width), BF),
            pltpu.VMEM((parts, rows, classes), BF),
            dma((3, 4)),
            dma((3, 4)),
            dma((af, CHUNKS)),
            dma((af, CHUNKS)),
            dma((af, CHUNKS)),
            dma((af,)),
            dma((af,)),
            dma((af,)),
            dma((af,)),
            dma((af,)),
            dma((af,)),
            dma((af, parts)),
            dma((af, parts)),
            dma((parts,)),
            dma((parts,)),
            dma((af,)),
            dma((af,)),
            dma((af, parts)),
            dma((af, parts)),
            dma((parts,)),
            dma((parts,)),
        ],
        compiler_params=pltpu.CompilerParams(
            collective_id=0, has_side_effects=True, vmem_limit_bytes=56 * 1024 * 1024
        ),
        name="gcn_step",
    )(
        features,
        adj_tiles,
        col_block.T,
        send_rows,
        send_counts,
        recv_target,
        edge_weight,
        labels.reshape(1, -1),
        w_hidden,
        w_classes,
    )
    return (
        grad_w.reshape(width, af * width).astype(F32),
        grad_c.reshape(width, classes).astype(F32),
    )


def solution(mesh):
    sizes = (mesh.shape["gx"], mesh.shape["gy"], mesh.shape["af"])
    placed = (
        P(("gx", "gy"), "af"),
        P(("gx", "gy"), None, None, None),
        P(("gx", "gy"), None),
        P(("gx", "gy"), None),
        P(("gx", "gy")),
        P(("gx", "gy"), None),
        P(("gx", "gy"), None),
        P(("gx", "gy")),
        P("af", None),
        P("af", None),
    )
    return jax.shard_map(
        functools.partial(local, sizes),
        mesh=mesh,
        in_specs=placed,
        out_specs=(P("af", None), P("af", None)),
        check_vma=False,
    )
```
